32 devices in a mesh: groups: 2 (over y), team: 4 (over z), rep: 4 (over x, core).
Axes of the slice: x: 2, y: 2, z: 4, core: 2. Of those that a mesh axis runs over, the one named last changes fastest.
Arguments:
- omega_rows: float32 [128, 32768], P(('groups', 'team'), 'rep'), parts along dimension 0, as said below
- covariance_columns: float32 [32768, 2048], P('rep', ('groups', 'team')), parts along dimension 1, may hold values from -0.03125 to 0.03125
- tile_offsets: int32 [8], P(('groups', 'team')), parts along dimension 0, may hold values from 0 to 32512, as said below
Outputs:
- new_omega: float32 [64, 2048], P('rep', ('groups', 'team')), parts along dimension 1
The draws below stay inside these ranges and needn't reach their ends.
There are 2 independent parts, one for each index of `groups`. The reference program is written for one: setup_inputs(seed, part) draws one part's arguments, and reference() takes and returns one part's arrays. A program takes and returns all parts, laid end to end along the dimension named above; each array names one. Nothing has to cross between parts.
Inputs may be any that keep to these rules, and one draw needn't show every extreme that they name: `tile_offsets`: distinct multiples of 256; both 0 and 32512 occur. `omega_rows`: entries with column equal to row lie in 1 to 2.
All inputs are finite; a program needn't handle non-finite values.
Results may differ from the reference program's by a relative error of at most 0.0003.
Values sent between devices are 32-bit elements; how exact they have to be, the bound alone decides.
A program may use at most 64 MiB of HBM per device.

```python
import jax
import jax.numpy as jnp
from jax import lax

P_SIZE = 32768
CB = 256
ROWS = 64
COLS = 1024
N_TEAM = 4


def draw_omega_rows(key, part):
    first_key = jax.random.fold_in(key, 11)
    second_key = jax.random.fold_in(key, 12)
    values = jax.random.normal(first_key, (ROWS, P_SIZE), jnp.float32)
    lifted = 1.0 + jax.random.uniform(second_key, (ROWS, P_SIZE), jnp.float32)
    row_ids = jnp.arange(ROWS, dtype=jnp.int32)[:, None]
    col_ids = jnp.arange(P_SIZE, dtype=jnp.int32)[None, :]
    return jnp.where(row_ids == col_ids, lifted, values)


def draw_tile_offsets(key, part):
    levels = P_SIZE // CB
    first_key = jax.random.fold_in(key, 21)
    second_key = jax.random.fold_in(key, 22)
    middle = jax.random.permutation(first_key, levels - 2)[:N_TEAM - 2] + 1
    chosen = jnp.concatenate([jnp.zeros((1,), jnp.int32), middle.astype(jnp.int32), jnp.full((1,), levels - 1, jnp.int32)])
    order = jax.random.permutation(second_key, N_TEAM)
    return (chosen[order] * CB).astype(jnp.int32)


def block_levels(stream_key, dims, pieces, least, top_value):
    gain = 1.0
    for position, shards_of in pieces:
        heights = jax.random.uniform(jax.random.fold_in(jax.random.fold_in(stream_key, 6), position), (shards_of,), jnp.float32, least / len(pieces), top_value / len(pieces))
        gain = gain * jnp.repeat(jnp.exp(heights), dims[position] // shards_of).reshape((-1,) + (1,) * (len(dims) - 1 - position))
    return gain


def normal_values(key, shape, spread, bound, split=(), kind=jnp.bfloat16):
    values = spread * jax.random.normal(key, shape, jnp.float32)
    if split:
        values = values * block_levels(key, shape, split, -0.22, 0.18)
    return jnp.clip(values, -bound, bound).astype(kind)


def setup_inputs(seed: int = 0, part: int = 0) -> dict:
    seeds = jax.random.split(jax.random.key(seed), 4)
    part_keys = jax.random.split(jax.random.fold_in(seeds[3], part), 4)
    omega_rows = draw_omega_rows(jax.random.fold_in(jax.random.fold_in(seeds[3], part), 71), part)
    covariance_columns = normal_values(part_keys[1], (P_SIZE, COLS), P_SIZE ** -0.5, 0.03125, ((0, 4), (1, 4)), jnp.float32)
    tile_offsets = draw_tile_offsets(jax.random.fold_in(jax.random.fold_in(seeds[3], part), 71), part)
    return {"omega_rows": omega_rows, "covariance_columns": covariance_columns, "tile_offsets": tile_offsets}


step_size = 0.5
penalty = 0.1


def reference(omega_rows, covariance_columns, tile_offsets):
    columns = (tile_offsets[:, None] + jnp.arange(CB, dtype=jnp.int32)[None, :]).reshape(-1).astype(jnp.int32)
    product = jnp.dot(omega_rows, covariance_columns, preferred_element_type=jnp.float32, precision=lax.Precision.HIGHEST)
    current = jnp.take(omega_rows, columns, axis=1)
    row_ids = jnp.arange(ROWS, dtype=jnp.int32)[:, None]
    diagonal = row_ids == columns[None, :]
    safe = jnp.where(diagonal, current, jnp.float32(1.0))
    gradient = product - jnp.where(diagonal, 1.0 / safe, jnp.float32(0.0))
    moved = current - step_size * gradient
    shrunk = jnp.sign(moved) * jnp.maximum(jnp.abs(moved) - step_size * penalty, 0.0)
    return jnp.where(diagonal, moved, shrunk)
```

```python
import functools

import jax
import jax.numpy as jnp
from jax import lax
from jax.experimental import pallas as pl
from jax.experimental.pallas import tpu as pltpu
from jax.sharding import PartitionSpec as P

MESH = pl.DeviceIdType.MESH
step_size = 0.5
penalty = 0.1


def kernel(teams, reps, chunks, omega, cov, offset, out, gath, stage, high, low, acc,
           current, part, inbox, cov_sem, own_sem, right_send, right_recv, left_send, left_recv, sum_send,
           sum_recv):
    t = lax.axis_index("team")
    r = lax.axis_index("rep")
    rows, width = omega.shape
    tile = cov.shape[1]
    piece = width // chunks
    share = teams * rows // reps

    def span(c):
        return pl.ds(pl.multiple_of(c * piece, piece), piece)

    def cov_copy(c):
        return pltpu.make_async_copy(cov.at[span(c), :], stage.at[span(c), :], cov_sem.at[c])

    own_copy = pltpu.make_async_copy(omega, gath.at[t], own_sem)
    own_copy.start()
    for c in range(chunks):
        cov_copy(c).start()

    barrier = pltpu.get_barrier_semaphore()

    @pl.when(t > 0)
    def _():
        pl.semaphore_signal(barrier, inc=1, device_id={"team": t - 1}, device_id_type=MESH)

    @pl.when(t < teams - 1)
    def _():
        pl.semaphore_signal(barrier, inc=1, device_id={"team": t + 1}, device_id_type=MESH)

    for d in range(1, reps):
        peer = lax.rem(r + d, reps)
        pl.semaphore_signal(barrier, inc=1, device_id={"rep": peer}, device_id_type=MESH)

    sides = jnp.where(t > 0, 1, 0) + jnp.where(t < teams - 1, 1, 0)
    pl.semaphore_wait(barrier, reps - 1 + sides)

    def send(way, q, own):
        block = t - (q // chunks) * way
        c = lax.rem(q, chunks)
        sems = (right_send, right_recv) if way > 0 else (left_send, left_recv)
        source = omega.at[:, span(c)] if own else gath.at[block, :, span(c)]
        return pltpu.make_async_remote_copy(
            src_ref=source, dst_ref=gath.at[block, :, span(c)],
            send_sem=sems[0].at[q], recv_sem=sems[1].at[q],
            device_id={"team": t + way}, device_id_type=MESH)

    def arrival(way, q):
        block = t - (q // chunks + 1) * way
        c = lax.rem(q, chunks)
        sems = (right_send, right_recv) if way > 0 else (left_send, left_recv)
        return pltpu.make_async_remote_copy(
            src_ref=gath.at[block, :, span(c)], dst_ref=gath.at[block, :, span(c)],
            send_sem=sems[0].at[q], recv_sem=sems[1].at[q],
            device_id={"team": t - way}, device_id_type=MESH)

    for c in range(chunks):
        @pl.when(t < teams - 1)
        def _():
            send(1, jnp.int32(c), True).start()

        @pl.when(t > 0)
        def _():
            send(-1, jnp.int32(c), True).start()

    acc[...] = jnp.zeros_like(acc)
    current[...] = jnp.zeros_like(current)
    origin = offset[0]

    def multiply(block, c):
        a = gath[block, :, span(c)]
        a_high = a.astype(jnp.bfloat16)
        a_low = (a - a_high.astype(jnp.float32)).astype(jnp.bfloat16)
        both = jnp.concatenate([a_high, a_low], axis=0)
        first = jnp.dot(both, high[span(c), :], preferred_element_type=jnp.float32)
        second = jnp.dot(both, low[span(c), :], preferred_element_type=jnp.float32)
        whole = first + second
        acc[pl.ds(pl.multiple_of(block * rows, rows), rows), :] += whole[:rows] + whole[rows:]
        found = jnp.zeros((rows, tile), jnp.float32)
        for k in range(piece // tile):
            begin = jnp.full((rows, tile), r * width + c * piece + k * tile, jnp.int32)
            found = found + jnp.where(begin == origin, a[:, k * tile:(k + 1) * tile], 0.0)
        current[pl.ds(pl.multiple_of(block * rows, rows), rows), :] += found

    own_copy.wait()

    @pl.loop(0, chunks)
    def _(c):
        cov_copy(c).wait()
        value = stage[span(c), :]
        top = value.astype(jnp.bfloat16)
        high[span(c), :] = top
        low[span(c), :] = (value - top.astype(jnp.float32)).astype(jnp.bfloat16)
        multiply(t, c)

    @pl.loop(0, (teams - 1) * chunks)
    def _(q):
        has_left = q < t * chunks
        has_right = q < (teams - 1 - t) * chunks

        @pl.when(has_left)
        def _():
            arrival(1, q).wait_recv()

            @pl.when(t < teams - 1)
            def _():
                send(1, q + chunks, False).start()

        @pl.when(has_right)
        def _():
            arrival(-1, q).wait_recv()

            @pl.when(t > 0)
            def _():
                send(-1, q + chunks, False).start()

        @pl.when(has_left)
        def _():
            multiply(t - 1 - q // chunks, lax.rem(q, chunks))

        @pl.when(has_right)
        def _():
            multiply(t + 1 + q // chunks, lax.rem(q, chunks))

    for s in range(teams):
        values = current[s * rows:(s + 1) * rows, :]
        row_ids = s * rows + lax.broadcasted_iota(jnp.int32, (rows, tile), 0)
        col_ids = origin + lax.broadcasted_iota(jnp.int32, (rows, tile), 1)
        mine = jnp.logical_and(col_ids >= r * width, col_ids < (r + 1) * width)
        diagonal = jnp.logical_and(row_ids == col_ids, mine)
        safe = jnp.where(diagonal, values, 1.0)
        kept = values + jnp.where(diagonal, step_size / safe, 0.0)
        part[s * rows:(s + 1) * rows, :] = kept - step_size * acc[s * rows:(s + 1) * rows, :]

    def exchange(d):
        peer = lax.rem(r + d, reps)
        return pltpu.make_async_remote_copy(
            src_ref=part.at[pl.ds(pl.multiple_of(peer * share, share), share), :],
            dst_ref=inbox.at[d - 1], send_sem=sum_send.at[d - 1], recv_sem=sum_recv.at[d - 1],
            device_id={"rep": peer}, device_id_type=MESH)

    for d in range(1, reps):
        exchange(d).start()
    total = part[pl.ds(pl.multiple_of(r * share, share), share), :]
    for d in range(1, reps):
        exchange(d).wait_recv()
        total = total + inbox[d - 1]
    out[...] = total

    for d in range(1, reps):
        exchange(d).wait_send()

    @pl.loop(0, teams * chunks)
    def _(q):
        @pl.when(jnp.logical_and(t < teams - 1, q < (t + 1) * chunks))
        def _():
            send(1, q, False).wait_send()

        @pl.when(jnp.logical_and(t > 0, q < (teams - t) * chunks))
        def _():
            send(-1, q, False).wait_send()


def per_device(teams, reps, omega_rows, covariance_columns, tile_offsets):
    rows, width = omega_rows.shape
    tile = covariance_columns.shape[1]
    share = rows * teams // reps
    chunks = max(1, min(32 // teams, width // 256))
    dma = pltpu.SemaphoreType.DMA
    moved = pl.pallas_call(
        functools.partial(kernel, teams, reps, chunks),
        out_shape=jax.ShapeDtypeStruct((share, tile), jnp.float32),
        in_specs=[
            pl.BlockSpec(memory_space=pl.ANY),
            pl.BlockSpec(memory_space=pl.ANY),
            pl.BlockSpec(memory_space=pltpu.SMEM),
        ],
        out_specs=pl.BlockSpec(memory_space=pltpu.VMEM),
        scratch_shapes=[
            pltpu.VMEM((teams, rows, width), jnp.float32),
            pltpu.VMEM((width, tile), jnp.float32),
            pltpu.VMEM((width, tile), jnp.bfloat16),
            pltpu.VMEM((width, tile), jnp.bfloat16),
            pltpu.VMEM((teams * rows, tile), jnp.float32),
            pltpu.VMEM((teams * rows, tile), jnp.float32),
            pltpu.VMEM((teams * rows, tile), jnp.float32),
            pltpu.VMEM((reps - 1, share, tile), jnp.float32),
            dma((chunks,)),
            dma,
            dma((teams * chunks,)),
            dma((teams * chunks,)),
            dma((teams * chunks,)),
            dma((teams * chunks,)),
            dma((reps - 1,)),
            dma((reps - 1,)),
        ],
        compiler_params=pltpu.CompilerParams(
            collective_id=0, has_side_effects=True, vmem_limit_bytes=48 * 1024 * 1024),
        cost_estimate=pl.CostEstimate(
            flops=8 * teams * rows * width * tile,
            bytes_accessed=4 * width * (tile + rows * teams), transcendentals=0),
    )(omega_rows, covariance_columns, tile_offsets)
    global_rows = lax.axis_index("rep") * share + jnp.arange(share, dtype=jnp.int32)
    global_cols = tile_offsets[0] + jnp.arange(tile, dtype=jnp.int32)
    diagonal = global_rows[:, None] == global_cols[None, :]
    shrunk = jnp.sign(moved) * jnp.maximum(jnp.abs(moved) - step_size * penalty, 0.0)
    return jnp.where(diagonal, moved, shrunk)


def solution(mesh):
    in_specs = (P(("groups", "team"), "rep"), P("rep", ("groups", "team")), P(("groups", "team")))
    out_specs = P("rep", ("groups", "team"))
    body = functools.partial(per_device, mesh.shape["team"], mesh.shape["rep"])
    return jax.shard_map(body, mesh=mesh, in_specs=in_specs, out_specs=out_specs, check_vma=False)
```

```python
import functools

import jax
import jax.numpy as jnp
from jax import lax
from jax.experimental import pallas as pl
from jax.experimental.pallas import tpu as pltpu
from jax.sharding import PartitionSpec as P

MESH = pl.DeviceIdType.MESH
step_size = 0.5
penalty = 0.1


def kernel(teams, reps, chunks, window, omega, cov, offset, out, gath, stage, high, low, acc,
           current, part, inbox, cov_sem, own_sem, right_send, right_recv, left_send, left_recv, sum_send,
           sum_recv, place, place_sem):
    t = lax.axis_index("team")
    r = lax.axis_index("rep")
    rows, width = omega.shape
    tile = cov.shape[1]
    piece = width // chunks
    share = teams * rows // reps

    def span(c):
        return pl.ds(pl.multiple_of(c * piece, piece), piece)

    def cov_copy(c):
        return pltpu.make_async_copy(cov.at[span(c), :], stage.at[span(c), :], cov_sem.at[c])

    own_copy = pltpu.make_async_copy(omega, gath.at[t], own_sem)
    own_copy.start()
    place_copy = pltpu.make_async_copy(offset, place, place_sem)
    place_copy.start()
    for c in range(chunks):
        cov_copy(c).start()

    barrier = pltpu.get_barrier_semaphore()

    @pl.when(t > 0)
    def _():
        pl.semaphore_signal(barrier, inc=1, device_id={"team": t - 1}, device_id_type=MESH)

    @pl.when(t < teams - 1)
    def _():
        pl.semaphore_signal(barrier, inc=1, device_id={"team": t + 1}, device_id_type=MESH)

    for d in range(1, reps):
        peer = lax.rem(r + d, reps)
        pl.semaphore_signal(barrier, inc=1, device_id={"rep": peer}, device_id_type=MESH)

    sides = jnp.where(t > 0, 1, 0) + jnp.where(t < teams - 1, 1, 0)
    pl.semaphore_wait(barrier, reps - 1 + sides)

    def send(way, q, own):
        block = t - (q // chunks) * way
        c = lax.rem(q, chunks)
        sems = (right_send, right_recv) if way > 0 else (left_send, left_recv)
        source = omega.at[:, span(c)] if own else gath.at[block, :, span(c)]
        return pltpu.make_async_remote_copy(
            src_ref=source, dst_ref=gath.at[block, :, span(c)],
            send_sem=sems[0].at[q], recv_sem=sems[1].at[q],
            device_id={"team": t + way}, device_id_type=MESH)

    def arrival(way, q):
        block = t - (q // chunks + 1) * way
        c = lax.rem(q, chunks)
        sems = (right_send, right_recv) if way > 0 else (left_send, left_recv)
        return pltpu.make_async_remote_copy(
            src_ref=gath.at[block, :, span(c)], dst_ref=gath.at[block, :, span(c)],
            send_sem=sems[0].at[q], recv_sem=sems[1].at[q],
            device_id={"team": t - way}, device_id_type=MESH)

    acc[...] = jnp.zeros_like(acc)
    current[...] = jnp.zeros_like(current)
    place_copy.wait()
    origin = place[0]

    def multiply(block, c):
        a = gath[block, :, span(c)]
        a_high = a.astype(jnp.bfloat16)
        a_low = (a - a_high.astype(jnp.float32)).astype(jnp.bfloat16)
        both = jnp.concatenate([a_high, a_low], axis=0)
        first = jnp.dot(both, high[span(c), :], preferred_element_type=jnp.float32)
        second = jnp.dot(both, low[span(c), :], preferred_element_type=jnp.float32)
        whole = first + second
        acc[pl.ds(pl.multiple_of(block * rows, rows), rows), :] += whole[:rows] + whole[rows:]
        found = jnp.zeros((rows, tile), jnp.float32)
        for k in range(piece // tile):
            begin = jnp.full((rows, tile), r * width + c * piece + k * tile, jnp.int32)
            found = found + jnp.where(begin == origin, a[:, k * tile:(k + 1) * tile], 0.0)
        current[pl.ds(pl.multiple_of(block * rows, rows), rows), :] += found

    own_copy.wait()

    def behind(way):
        return t if way > 0 else teams - 1 - t

    def forward(way, q):
        sends = jnp.logical_and(behind(-way) > 0, q < (behind(way) + 1) * chunks)

        @pl.when(jnp.logical_and(q >= chunks, q < (behind(way) + 1) * chunks))
        def _():
            arrival(way, q - chunks).wait_recv()

        @pl.when(jnp.logical_and(sends, q >= window))
        def _():
            send(way, q - window, False).wait_send()

        @pl.when(jnp.logical_and(sends, q < chunks))
        def _():
            send(way, q, True).start()

        @pl.when(jnp.logical_and(sends, q >= chunks))
        def _():
            send(way, q, False).start()

    @pl.loop(0, teams * chunks)
    def _(q):
        forward(1, q)
        forward(-1, q)

        @pl.when(q < chunks)
        def _():
            cov_copy(q).wait()
            value = stage[span(q), :]
            top = value.astype(jnp.bfloat16)
            high[span(q), :] = top
            low[span(q), :] = (value - top.astype(jnp.float32)).astype(jnp.bfloat16)
            multiply(t, q)

        for way in (1, -1):
            @pl.when(jnp.logical_and(q >= chunks, q < (behind(way) + 1) * chunks))
            def _():
                multiply(t - way * (q // chunks), lax.rem(q, chunks))

    for s in range(teams):
        values = current[s * rows:(s + 1) * rows, :]
        row_ids = s * rows + lax.broadcasted_iota(jnp.int32, (rows, tile), 0)
        col_ids = origin + lax.broadcasted_iota(jnp.int32, (rows, tile), 1)
        mine = jnp.logical_and(col_ids >= r * width, col_ids < (r + 1) * width)
        diagonal = jnp.logical_and(row_ids == col_ids, mine)
        safe = jnp.where(diagonal, values, 1.0)
        kept = values + jnp.where(diagonal, step_size / safe, 0.0)
        part[s * rows:(s + 1) * rows, :] = kept - step_size * acc[s * rows:(s + 1) * rows, :]

    def exchange(d):
        peer = lax.rem(r + d, reps)
        return pltpu.make_async_remote_copy(
            src_ref=part.at[pl.ds(pl.multiple_of(peer * share, share), share), :],
            dst_ref=inbox.at[d - 1], send_sem=sum_send.at[d - 1], recv_sem=sum_recv.at[d - 1],
            device_id={"rep": peer}, device_id_type=MESH)

    for d in range(1, reps):
        exchange(d).start()
    total = part[pl.ds(pl.multiple_of(r * share, share), share), :]
    for d in range(1, reps):
        exchange(d).wait_recv()
        total = total + inbox[d - 1]
    out[...] = total

    for d in range(1, reps):
        exchange(d).wait_send()

    for way in (1, -1):
        for w in range(1, window + 1):
            @pl.when(behind(-way) > 0)
            def _():
                send(way, (behind(way) + 1) * chunks - w, False).wait_send()


def per_device(teams, reps, omega_rows, covariance_columns, tile_offsets):
    rows, width = omega_rows.shape
    tile = covariance_columns.shape[1]
    share = rows * teams // reps
    chunks = max(1, min(16 // teams, width // 256))
    dma = pltpu.SemaphoreType.DMA
    moved = pl.pallas_call(
        functools.partial(kernel, teams, reps, chunks, min(2, chunks)),
        out_shape=jax.ShapeDtypeStruct((share, tile), jnp.float32),
        in_specs=[
            pl.BlockSpec(memory_space=pl.ANY),
            pl.BlockSpec(memory_space=pl.ANY),
            pl.BlockSpec(memory_space=pl.ANY),
        ],
        out_specs=pl.BlockSpec(memory_space=pltpu.VMEM),
        scratch_shapes=[
            pltpu.VMEM((teams, rows, width), jnp.float32),
            pltpu.VMEM((width, tile), jnp.float32),
            pltpu.VMEM((width, tile), jnp.bfloat16),
            pltpu.VMEM((width, tile), jnp.bfloat16),
            pltpu.VMEM((teams * rows, tile), jnp.float32),
            pltpu.VMEM((teams * rows, tile), jnp.float32),
            pltpu.VMEM((teams * rows, tile), jnp.float32),
            pltpu.VMEM((reps - 1, share, tile), jnp.float32),
            dma((chunks,)),
            dma,
            dma((teams * chunks,)),
            dma((teams * chunks,)),
            dma((teams * chunks,)),
            dma((teams * chunks,)),
            dma((reps - 1,)),
            dma((reps - 1,)),
            pltpu.SMEM((1,), jnp.int32),
            dma,
        ],
        compiler_params=pltpu.CompilerParams(
            collective_id=0, has_side_effects=True, vmem_limit_bytes=63_000_000),
        cost_estimate=pl.CostEstimate(
            flops=8 * teams * rows * width * tile,
            bytes_accessed=4 * width * (tile + rows * teams), transcendentals=0),
    )(omega_rows, covariance_columns, tile_offsets)
    global_rows = lax.axis_index("rep") * share + jnp.arange(share, dtype=jnp.int32)
    global_cols = tile_offsets[0] + jnp.arange(tile, dtype=jnp.int32)
    diagonal = global_rows[:, None] == global_cols[None, :]
    shrunk = jnp.sign(moved) * jnp.maximum(jnp.abs(moved) - step_size * penalty, 0.0)
    return jnp.where(diagonal, moved, shrunk)


def solution(mesh):
    in_specs = (P(("groups", "team"), "rep"), P("rep", ("groups", "team")), P(("groups", "team")))
    out_specs = P("rep", ("groups", "team"))
    body = functools.partial(per_device, mesh.shape["team"], mesh.shape["rep"])
    return jax.shard_map(body, mesh=mesh, in_specs=in_specs, out_specs=out_specs, check_vma=False)
```

```python
import functools

import jax
import jax.numpy as jnp
from jax import lax
from jax.experimental import pallas as pl
from jax.experimental.pallas import tpu as pltpu
from jax.sharding import PartitionSpec as P

MESH = pl.DeviceIdType.MESH
step_size = 0.5
penalty = 0.1


def kernel(teams, reps, widths, lend, omega, cov, offset, out, gath, stage, high, low, acc,
           current, part, inbox, loan, repaid, reply, note_out, note_in, cov_sem, own_sem,
           right_send, right_recv, left_send, left_recv, sum_send, sum_recv, place, place_sem,
           lend_send, lend_recv):
    t = lax.axis_index("team")
    r = lax.axis_index("rep")
    rows, width = omega.shape
    tile = cov.shape[1]
    chunks = len(widths)
    lent = widths[0]
    share = teams * rows // reps

    def span(c):
        return pl.ds(sum(widths[:c]), widths[c])

    def cov_copy(c):
        return pltpu.make_async_copy(cov.at[span(c), :], stage.at[span(c), :], cov_sem.at[c])

    def behind(way):
        return t if way > 0 else teams - 1 - t

    def ahead(way):
        return behind(-way)

    own_copy = pltpu.make_async_copy(omega, gath.at[t], own_sem)
    own_copy.start()
    place_copy = pltpu.make_async_copy(offset, place, place_sem)
    place_copy.start()
    for c in range(chunks):
        cov_copy(c).start()

    barrier = pltpu.get_barrier_semaphore()

    @pl.when(t > 0)
    def _():
        pl.semaphore_signal(barrier, inc=1, device_id={"team": t - 1}, device_id_type=MESH)

    @pl.when(t < teams - 1)
    def _():
        pl.semaphore_signal(barrier, inc=1, device_id={"team": t + 1}, device_id_type=MESH)

    for d in range(1, reps):
        peer = lax.rem(r + d, reps)
        pl.semaphore_signal(barrier, inc=1, device_id={"rep": peer}, device_id_type=MESH)

    sides = jnp.where(t > 0, 1, 0) + jnp.where(t < teams - 1, 1, 0)
    pl.semaphore_wait(barrier, reps - 1 + sides)

    def send(way, j, c):
        q = j * chunks + c
        sems = (right_send, right_recv) if way > 0 else (left_send, left_recv)
        view = gath.at[t - j * way, :, span(c)]
        return pltpu.make_async_remote_copy(
            src_ref=view, dst_ref=view, send_sem=sems[0].at[q], recv_sem=sems[1].at[q],
            device_id={"team": t + way}, device_id_type=MESH)

    def arrival(way, j, c):
        q = j * chunks + c
        sems = (right_send, right_recv) if way > 0 else (left_send, left_recv)
        view = gath.at[t - (j + 1) * way, :, span(c)]
        return pltpu.make_async_remote_copy(
            src_ref=view, dst_ref=view, send_sem=sems[0].at[q], recv_sem=sems[1].at[q],
            device_id={"team": t - way}, device_id_type=MESH)

    def sends(way, j, c):
        least = 1 if lend and c == 0 else 0
        return jnp.logical_and(ahead(way) > least, j <= behind(way))

    def receives(way, j, c):
        wanted = jnp.logical_and(j >= 1, j <= behind(way))
        if lend and c == 0:
            wanted = jnp.logical_and(wanted, ahead(way) > 0)
        return wanted

    def towards(way, source, target, index):
        return pltpu.make_async_remote_copy(
            src_ref=source, dst_ref=target, send_sem=lend_send.at[index],
            recv_sem=lend_recv.at[index], device_id={"team": t + way}, device_id_type=MESH)

    def loan_copy(way):
        return towards(way, cov.at[pl.ds(0, lent), :], loan, 0)

    def note_copy(way):
        return towards(way, note_out, note_in, 1)

    def reply_copy(way):
        others = pl.ds(0 if way > 0 else rows, (teams - 1) * rows)
        return towards(way, reply.at[others, :], repaid.at[others, :], 2)

    place_copy.wait()
    origin = place[0]
    if lend:
        repaid[...] = jnp.zeros_like(repaid)
        note_out[...] = jnp.full(note_out.shape, origin, jnp.int32).astype(jnp.float32)
        for way in (1, -1):
            @pl.when(ahead(way) == 0)
            def _():
                loan_copy(-way).start()
                note_copy(-way).start()

    acc[...] = jnp.zeros_like(acc)
    current[...] = jnp.zeros_like(current)

    def halves(value):
        top = value.astype(jnp.bfloat16)
        return top, (value - top.astype(jnp.float32)).astype(jnp.bfloat16)

    def product(a, b_high, b_low):
        both = jnp.concatenate(halves(a), axis=0)
        whole = jnp.dot(both, b_high, preferred_element_type=jnp.float32)
        whole = whole + jnp.dot(both, b_low, preferred_element_type=jnp.float32)
        return whole[:a.shape[0]] + whole[a.shape[0]:]

    def found(a, begin, where):
        total = jnp.zeros((a.shape[0], tile), jnp.float32)
        for k in range(a.shape[1] // tile):
            here = jnp.full((a.shape[0], tile), begin + k * tile, jnp.int32)
            total = total + jnp.where(here == where, a[:, k * tile:(k + 1) * tile], 0.0)
        return total

    def combined(values, products, first_row, where, low_col, high_col):
        row_ids = first_row + lax.broadcasted_iota(jnp.int32, values.shape, 0)
        col_ids = where + lax.broadcasted_iota(jnp.int32, values.shape, 1)
        mine = jnp.logical_and(col_ids >= low_col, col_ids < high_col)
        diagonal = jnp.logical_and(row_ids == col_ids, mine)
        safe = jnp.where(diagonal, values, 1.0)
        return values + jnp.where(diagonal, step_size / safe, 0.0) - step_size * products

    def multiply(block, c):
        a = gath[block, :, span(c)]
        place_rows = pl.ds(pl.multiple_of(block * rows, rows), rows)
        acc[place_rows, :] += product(a, high[span(c), :], low[span(c), :])
        current[place_rows, :] += found(a, r * width + sum(widths[:c]), origin)

    own_copy.wait()

    @pl.loop(0, teams)
    def _(j):
        for c in range(chunks):
            for way in (1, -1):
                @pl.when(receives(way, j, c))
                def _():
                    arrival(way, j - 1, c).wait_recv()

                ready = sends(way, j, c)
                if c > 0:
                    ready = jnp.logical_and(ready, j >= 1)

                @pl.when(ready)
                def _():
                    send(way, j, c).start()

            if c == 0:
                @pl.when(j == 0)
                def _():
                    for n in range(1, chunks):
                        for way in (1, -1):
                            @pl.when(sends(way, j, n))
                            def _():
                                send(way, j, n).start()

            @pl.when(j == 0)
            def _():
                cov_copy(c).wait()
                top, rest = halves(stage[span(c), :])
                high[span(c), :] = top
                low[span(c), :] = rest
                multiply(t, c)

            for way in (1, -1):
                @pl.when(receives(way, j, c))
                def _():
                    multiply(t - way * j, c)

    if lend:
        for way in (1, -1):
            @pl.when(ahead(way) == 1)
            def _():
                loan_copy(-way).wait_recv()
                note_copy(-way).wait_recv()
                where = note_in[0:1, :].astype(jnp.int32)
                top, rest = halves(loan[...])
                for n in range(teams - 1):
                    block = n if way > 0 else n + 1
                    a = gath[block, :, span(0)]
                    reply[block * rows:(block + 1) * rows, :] = combined(
                        found(a, r * width, where), product(a, top, rest), block * rows, where,
                        r * width, r * width + lent)
                reply_copy(way).start()

    is_end = jnp.logical_or(t == 0, t == teams - 1)
    for s in range(teams):
        low_col = r * width
        if lend:
            low_col = low_col + jnp.where(jnp.logical_and(is_end, t != s), lent, 0)
        block = slice(s * rows, (s + 1) * rows)
        part[block, :] = combined(
            current[block, :], acc[block, :], s * rows, origin, low_col, (r + 1) * width)

    if lend:
        for way in (1, -1):
            @pl.when(ahead(way) == 0)
            def _():
                reply_copy(-way).wait_recv()
                part[...] += repaid[...]

    def exchange(d):
        peer = lax.rem(r + d, reps)
        return pltpu.make_async_remote_copy(
            src_ref=part.at[pl.ds(pl.multiple_of(peer * share, share), share), :],
            dst_ref=inbox.at[d - 1], send_sem=sum_send.at[d - 1], recv_sem=sum_recv.at[d - 1],
            device_id={"rep": peer}, device_id_type=MESH)

    for d in range(1, reps):
        exchange(d).start()
    total = part[pl.ds(pl.multiple_of(r * share, share), share), :]
    for d in range(1, reps):
        exchange(d).wait_recv()
        total = total + inbox[d - 1]
    out[...] = total

    for d in range(1, reps):
        exchange(d).wait_send()

    for way in (1, -1):
        if lend:
            @pl.when(ahead(way) == 0)
            def _():
                loan_copy(-way).wait_send()
                note_copy(-way).wait_send()

            @pl.when(ahead(way) == 1)
            def _():
                reply_copy(way).wait_send()

        @pl.loop(0, teams)
        def _(j):
            for c in range(chunks):
                @pl.when(sends(way, j, c))
                def _():
                    send(way, j, c).wait_send()


def per_device(teams, reps, omega_rows, covariance_columns, tile_offsets):
    rows, width = omega_rows.shape
    tile = covariance_columns.shape[1]
    share = rows * teams // reps
    units = width // tile
    lend = teams >= 4 and units >= 8
    exact = units * (teams - 2) * rows // ((teams - 1) * rows + tile)
    lent = max(1, min(exact, units // 8))
    long = max(1, (units - lent) * 3 // 7)
    widths = [n * tile for n in (lent, long, long, units - lent - 2 * long)]
    chunks = len(widths)
    dma = pltpu.SemaphoreType.DMA
    moved = pl.pallas_call(
        functools.partial(kernel, teams, reps, widths, lend),
        out_shape=jax.ShapeDtypeStruct((share, tile), jnp.float32),
        in_specs=[
            pl.BlockSpec(memory_space=pl.ANY),
            pl.BlockSpec(memory_space=pl.ANY),
            pl.BlockSpec(memory_space=pl.ANY),
        ],
        out_specs=pl.BlockSpec(memory_space=pltpu.VMEM),
        scratch_shapes=[
            pltpu.VMEM((teams, rows, width), jnp.float32),
            pltpu.VMEM((width, tile), jnp.float32),
            pltpu.VMEM((width, tile), jnp.bfloat16),
            pltpu.VMEM((width, tile), jnp.bfloat16),
            pltpu.VMEM((teams * rows, tile), jnp.float32),
            pltpu.VMEM((teams * rows, tile), jnp.float32),
            pltpu.VMEM((teams * rows, tile), jnp.float32),
            pltpu.VMEM((reps - 1, share, tile), jnp.float32),
            pltpu.VMEM((widths[0], tile), jnp.float32),
            pltpu.VMEM((teams * rows, tile), jnp.float32),
            pltpu.VMEM((teams * rows, tile), jnp.float32),
            pltpu.VMEM((8, tile), jnp.float32),
            pltpu.VMEM((8, tile), jnp.float32),
            dma((chunks,)),
            dma,
            dma((teams * chunks,)),
            dma((teams * chunks,)),
            dma((teams * chunks,)),
            dma((teams * chunks,)),
            dma((reps - 1,)),
            dma((reps - 1,)),
            pltpu.SMEM((1,), jnp.int32),
            dma,
            dma((3,)),
            dma((3,)),
        ],
        compiler_params=pltpu.CompilerParams(
            collective_id=0, has_side_effects=True, vmem_limit_bytes=50_000_000),
        cost_estimate=pl.CostEstimate(
            flops=8 * teams * rows * width * tile,
            bytes_accessed=4 * width * (tile + rows * teams), transcendentals=0),
    )(omega_rows, covariance_columns, tile_offsets)
    global_rows = lax.axis_index("rep") * share + jnp.arange(share, dtype=jnp.int32)
    global_cols = tile_offsets[0] + jnp.arange(tile, dtype=jnp.int32)
    diagonal = global_rows[:, None] == global_cols[None, :]
    shrunk = jnp.sign(moved) * jnp.maximum(jnp.abs(moved) - step_size * penalty, 0.0)
    return jnp.where(diagonal, moved, shrunk)


def solution(mesh):
    in_specs = (P(("groups", "team"), "rep"), P("rep", ("groups", "team")), P(("groups", "team")))
    out_specs = P("rep", ("groups", "team"))
    body = functools.partial(per_device, mesh.shape["team"], mesh.shape["rep"])
    return jax.shard_map(body, mesh=mesh, in_specs=in_specs, out_specs=out_specs, check_vma=False)
```

```python
import functools

import jax
import jax.numpy as jnp
from jax import lax
from jax.experimental import pallas as pl
from jax.experimental.pallas import tpu as pltpu
from jax.sharding import PartitionSpec as P

MESH = pl.DeviceIdType.MESH
step_size = 0.5
penalty = 0.1


def kernel(teams, reps, widths, lend, omega, cov, offset, out, gath, stage, high, low, acc,
           current, part, inbox, loan, repaid, reply, note_out, note_in, cov_sem, own_sem,
           right_send, right_recv, left_send, left_recv, sum_send, sum_recv, place, place_sem,
           lend_send, lend_recv):
    t = lax.axis_index("team")
    r = lax.axis_index("rep")
    rows, width = omega.shape
    tile = cov.shape[1]
    chunks = len(widths)
    lent = widths[0]
    share = teams * rows // reps

    def span(c):
        return pl.ds(sum(widths[:c]), widths[c])

    def cov_copy(c):
        return pltpu.make_async_copy(cov.at[span(c), :], stage.at[span(c), :], cov_sem.at[c])

    def behind(way):
        return t if way > 0 else teams - 1 - t

    def ahead(way):
        return behind(-way)

    own_copy = pltpu.make_async_copy(omega, gath.at[t], own_sem)
    own_copy.start()
    place_copy = pltpu.make_async_copy(offset, place, place_sem)
    place_copy.start()
    for c in range(chunks):
        cov_copy(c).start()

    barrier = pltpu.get_barrier_semaphore()

    @pl.when(t > 0)
    def _():
        pl.semaphore_signal(barrier, inc=1, device_id={"team": t - 1}, device_id_type=MESH)

    @pl.when(t < teams - 1)
    def _():
        pl.semaphore_signal(barrier, inc=1, device_id={"team": t + 1}, device_id_type=MESH)

    for d in range(1, reps):
        peer = lax.rem(r + d, reps)
        pl.semaphore_signal(barrier, inc=1, device_id={"rep": peer}, device_id_type=MESH)

    sides = jnp.where(t > 0, 1, 0) + jnp.where(t < teams - 1, 1, 0)
    pl.semaphore_wait(barrier, reps - 1 + sides)

    def send(way, j, c):
        q = j * chunks + c
        sems = (right_send, right_recv) if way > 0 else (left_send, left_recv)
        view = gath.at[t - j * way, :, span(c)]
        return pltpu.make_async_remote_copy(
            src_ref=view, dst_ref=view, send_sem=sems[0].at[q], recv_sem=sems[1].at[q],
            device_id={"team": t + way}, device_id_type=MESH)

    def arrival(way, j, c):
        q = j * chunks + c
        sems = (right_send, right_recv) if way > 0 else (left_send, left_recv)
        view = gath.at[t - (j + 1) * way, :, span(c)]
        return pltpu.make_async_remote_copy(
            src_ref=view, dst_ref=view, send_sem=sems[0].at[q], recv_sem=sems[1].at[q],
            device_id={"team": t - way}, device_id_type=MESH)

    def sends(way, j, c):
        least = 1 if lend and c == 0 else 0
        return jnp.logical_and(ahead(way) > least, j <= behind(way))

    def receives(way, j, c):
        wanted = jnp.logical_and(j >= 1, j <= behind(way))
        if lend and c == 0:
            wanted = jnp.logical_and(wanted, ahead(way) > 0)
        return wanted

    def towards(way, source, target, index):
        return pltpu.make_async_remote_copy(
            src_ref=source, dst_ref=target, send_sem=lend_send.at[index],
            recv_sem=lend_recv.at[index], device_id={"team": t + way}, device_id_type=MESH)

    def loan_copy(way):
        return towards(way, cov.at[pl.ds(0, lent), :], loan, 0)

    def note_copy(way):
        return towards(way, note_out, note_in, 1)

    def reply_copy(way):
        others = pl.ds(0 if way > 0 else rows, (teams - 1) * rows)
        return towards(way, reply.at[others, :], repaid.at[others, :], 2)

    place_copy.wait()
    origin = place[0]
    if lend:
        repaid[...] = jnp.zeros_like(repaid)
        note_out[...] = jnp.full(note_out.shape, origin, jnp.int32).astype(jnp.float32)

    acc[...] = jnp.zeros_like(acc)
    current[...] = jnp.zeros_like(current)

    def halves(value):
        top = value.astype(jnp.bfloat16)
        return top, (value - top.astype(jnp.float32)).astype(jnp.bfloat16)

    def product(a, b_high, b_low):
        both = jnp.concatenate(halves(a), axis=0)
        whole = jnp.dot(both, b_high, preferred_element_type=jnp.float32)
        whole = whole + jnp.dot(both, b_low, preferred_element_type=jnp.float32)
        return whole[:a.shape[0]] + whole[a.shape[0]:]

    def found(a, begin, where):
        total = jnp.zeros((a.shape[0], tile), jnp.float32)
        for k in range(a.shape[1] // tile):
            here = jnp.full((a.shape[0], tile), begin + k * tile, jnp.int32)
            total = total + jnp.where(here == where, a[:, k * tile:(k + 1) * tile], 0.0)
        return total

    def combined(values, products, first_row, where, low_col, high_col):
        row_ids = first_row + lax.broadcasted_iota(jnp.int32, values.shape, 0)
        col_ids = where + lax.broadcasted_iota(jnp.int32, values.shape, 1)
        mine = jnp.logical_and(col_ids >= low_col, col_ids < high_col)
        diagonal = jnp.logical_and(row_ids == col_ids, mine)
        safe = jnp.where(diagonal, values, 1.0)
        return values + jnp.where(diagonal, step_size / safe, 0.0) - step_size * products

    def multiply(block, c):
        a = gath[block, :, span(c)]
        place_rows = pl.ds(pl.multiple_of(block * rows, rows), rows)
        acc[place_rows, :] += product(a, high[span(c), :], low[span(c), :])
        current[place_rows, :] += found(a, r * width + sum(widths[:c]), origin)

    own_copy.wait()

    @pl.loop(0, teams)
    def _(j):
        for c in range(chunks):
            for way in (1, -1):
                @pl.when(receives(way, j, c))
                def _():
                    arrival(way, j - 1, c).wait_recv()

                ready = sends(way, j, c)
                if c > 0:
                    ready = jnp.logical_and(ready, j >= 1)

                @pl.when(ready)
                def _():
                    send(way, j, c).start()

            if c == 0:
                @pl.when(j == 0)
                def _():
                    for n in range(1, chunks):
                        for way in (1, -1):
                            @pl.when(sends(way, j, n))
                            def _():
                                send(way, j, n).start()

            if lend and c == 0:
                @pl.when(j == 0)
                def _():
                    for way in (1, -1):
                        @pl.when(ahead(way) == 0)
                        def _():
                            loan_copy(-way).start()
                            note_copy(-way).start()

            @pl.when(j == 0)
            def _():
                cov_copy(c).wait()
                top, rest = halves(stage[span(c), :])
                high[span(c), :] = top
                low[span(c), :] = rest
                multiply(t, c)

            for way in (1, -1):
                @pl.when(receives(way, j, c))
                def _():
                    multiply(t - way * j, c)

    if lend:
        for way in (1, -1):
            @pl.when(ahead(way) == 1)
            def _():
                loan_copy(-way).wait_recv()
                note_copy(-way).wait_recv()
                where = note_in[0:1, :].astype(jnp.int32)
                top, rest = halves(loan[...])
                for n in range(teams - 1):
                    block = n if way > 0 else n + 1
                    a = gath[block, :, span(0)]
                    reply[block * rows:(block + 1) * rows, :] = combined(
                        found(a, r * width, where), product(a, top, rest), block * rows, where,
                        r * width, r * width + lent)
                reply_copy(way).start()

    is_end = jnp.logical_or(t == 0, t == teams - 1)
    for s in range(teams):
        low_col = r * width
        if lend:
            low_col = low_col + jnp.where(jnp.logical_and(is_end, t != s), lent, 0)
        block = slice(s * rows, (s + 1) * rows)
        part[block, :] = combined(
            current[block, :], acc[block, :], s * rows, origin, low_col, (r + 1) * width)

    if lend:
        for way in (1, -1):
            @pl.when(ahead(way) == 0)
            def _():
                reply_copy(-way).wait_recv()
                part[...] += repaid[...]

    def exchange(d):
        peer = lax.rem(r + d, reps)
        return pltpu.make_async_remote_copy(
            src_ref=part.at[pl.ds(pl.multiple_of(peer * share, share), share), :],
            dst_ref=inbox.at[d - 1], send_sem=sum_send.at[d - 1], recv_sem=sum_recv.at[d - 1],
            device_id={"rep": peer}, device_id_type=MESH)

    for d in range(1, reps):
        exchange(d).start()
    total = part[pl.ds(pl.multiple_of(r * share, share), share), :]
    for d in range(1, reps):
        exchange(d).wait_recv()
        total = total + inbox[d - 1]
    out[...] = total

    for d in range(1, reps):
        exchange(d).wait_send()

    for way in (1, -1):
        if lend:
            @pl.when(ahead(way) == 0)
            def _():
                loan_copy(-way).wait_send()
                note_copy(-way).wait_send()

            @pl.when(ahead(way) == 1)
            def _():
                reply_copy(way).wait_send()

        @pl.loop(0, teams)
        def _(j):
            for c in range(chunks):
                @pl.when(sends(way, j, c))
                def _():
                    send(way, j, c).wait_send()


def per_device(teams, reps, omega_rows, covariance_columns, tile_offsets):
    rows, width = omega_rows.shape
    tile = covariance_columns.shape[1]
    share = rows * teams // reps
    units = width // tile
    lend = teams >= 4 and units >= 8
    exact = units * (teams - 2) * rows // ((teams - 1) * rows + tile)
    lent = max(1, min(exact, units // 8))
    long = max(1, (units - lent) * 3 // 7)
    widths = [n * tile for n in (lent, long, long, units - lent - 2 * long)]
    chunks = len(widths)
    dma = pltpu.SemaphoreType.DMA
    moved = pl.pallas_call(
        functools.partial(kernel, teams, reps, widths, lend),
        out_shape=jax.ShapeDtypeStruct((share, tile), jnp.float32),
        in_specs=[
            pl.BlockSpec(memory_space=pl.ANY),
            pl.BlockSpec(memory_space=pl.ANY),
            pl.BlockSpec(memory_space=pl.ANY),
        ],
        out_specs=pl.BlockSpec(memory_space=pltpu.VMEM),
        scratch_shapes=[
            pltpu.VMEM((teams, rows, width), jnp.float32),
            pltpu.VMEM((width, tile), jnp.float32),
            pltpu.VMEM((width, tile), jnp.bfloat16),
            pltpu.VMEM((width, tile), jnp.bfloat16),
            pltpu.VMEM((teams * rows, tile), jnp.float32),
            pltpu.VMEM((teams * rows, tile), jnp.float32),
            pltpu.VMEM((teams * rows, tile), jnp.float32),
            pltpu.VMEM((reps - 1, share, tile), jnp.float32),
            pltpu.VMEM((widths[0], tile), jnp.float32),
            pltpu.VMEM((teams * rows, tile), jnp.float32),
            pltpu.VMEM((teams * rows, tile), jnp.float32),
            pltpu.VMEM((8, tile), jnp.float32),
            pltpu.VMEM((8, tile), jnp.float32),
            dma((chunks,)),
            dma,
            dma((teams * chunks,)),
            dma((teams * chunks,)),
            dma((teams * chunks,)),
            dma((teams * chunks,)),
            dma((reps - 1,)),
            dma((reps - 1,)),
            pltpu.SMEM((1,), jnp.int32),
            dma,
            dma((3,)),
            dma((3,)),
        ],
        compiler_params=pltpu.CompilerParams(
            collective_id=0, has_side_effects=True, vmem_limit_bytes=50_000_000),
        cost_estimate=pl.CostEstimate(
            flops=8 * teams * rows * width * tile,
            bytes_accessed=4 * width * (tile + rows * teams), transcendentals=0),
    )(omega_rows, covariance_columns, tile_offsets)
    global_rows = lax.axis_index("rep") * share + jnp.arange(share, dtype=jnp.int32)
    global_cols = tile_offsets[0] + jnp.arange(tile, dtype=jnp.int32)
    diagonal = global_rows[:, None] == global_cols[None, :]
    shrunk = jnp.sign(moved) * jnp.maximum(jnp.abs(moved) - step_size * penalty, 0.0)
    return jnp.where(diagonal, moved, shrunk)


def solution(mesh):
    in_specs = (P(("groups", "team"), "rep"), P("rep", ("groups", "team")), P(("groups", "team")))
    out_specs = P("rep", ("groups", "team"))
    body = functools.partial(per_device, mesh.shape["team"], mesh.shape["rep"])
    return jax.shard_map(body, mesh=mesh, in_specs=in_specs, out_specs=out_specs, check_vma=False)
```
